128 devices in a mesh: dp: 16 (over y_lo, x, core), tensor: 8 (over z, y_hi).
Axes of the slice: x: 4, y: 4 (y_hi: 2, y_lo: 2; y = y_hi * 2 + y_lo), z: 4, core: 2. Of those that a mesh axis runs over, the one named last changes fastest.
Arguments:
- hidden: bfloat16 [128, 16384], P('dp'), may hold values from -6 to 6
- norm_gain: bfloat16 [16384], replicated, may hold values from 0.099609375 to 1.8984375
- query_weight: bfloat16 [16384, 16384], P('dp', 'tensor'), may hold values from -0.046875 to 0.046875
- keyval_weight: bfloat16 [16384, 8, 256], P('dp', 'tensor'), may hold values from -0.046875 to 0.046875
- output_weight: bfloat16 [16384, 16384], P('tensor', 'dp'), may hold values from -0.046875 to 0.046875
- kv_cache: bfloat16 [128, 8, 1024, 256], P('dp', 'tensor')
- cache_lengths: int32 [128], P('dp'), may hold values from 128 to 1024, as said below
- next_source: bfloat16 [128, 128, 16384], P(('dp', 'tensor')), may hold values from -0.046875 to 0.046875
- block_ids: int32 [128], P('dp'), may hold values from 0 to 127, as said below
Outputs:
- mixed: bfloat16 [128, 16384], P('dp')
- next_weight: bfloat16 [16384, 16384], P('dp', 'tensor')
The draws below stay inside these ranges and needn't reach their ends.
Inputs may be any that keep to these rules, and one draw needn't show every extreme that they name: `cache_lengths`: some row uses exactly 1024 positions. `block_ids`: a permutation; the 8 entries on one dp index name at most 1 block within the rows of any one dp index, and that many for some.
All inputs are finite; a program needn't handle non-finite values.
Results may differ from the reference program's by a relative error of at most 0.04.
Values may be sent and summed in bfloat16 or wider, within the bound.
No kernel may reach another device: no remote copies, remote signals or barrier semaphores. Data moves between devices by JAX's collectives and lax.ppermute only.
A program may use at most 128 MiB of HBM per device.

```python
import jax
import jax.numpy as jnp
from jax import lax

D = 16384
KV_HEADS = 8
HEAD_DIM = 128
CACHE = 1024
BLOCK_ROWS = 128
ROWS = 128
QCOLS = 16384
NBLK = 128
GROUP_BLOCKS = 8


def draw_kv_cache(key, part):
    key = jax.random.fold_in(key, 7)
    values = jax.random.normal(key, (ROWS, KV_HEADS, CACHE, 2 * HEAD_DIM), jnp.float32)
    return values.astype(jnp.bfloat16)


def draw_cache_lengths(key, part):
    key = jax.random.fold_in(key, 5)
    length_key, row_key = jax.random.split(key)
    lengths = jax.random.randint(length_key, (ROWS,), CACHE // 8, CACHE + 1)
    chosen = jax.random.randint(row_key, (), 0, ROWS)
    return jnp.where(jnp.arange(ROWS) == chosen, CACHE, lengths).astype(jnp.int32)


def draw_block_ids(key, part):
    key = jax.random.fold_in(key, 11)
    groups = NBLK // GROUP_BLOCKS
    offset_key, order_key, shuffle_key = jax.random.split(key, 3)
    offset = jax.random.permutation(offset_key, groups).astype(jnp.int32)
    slots = jnp.arange(GROUP_BLOCKS, dtype=jnp.int32)
    target = ((slots[None, :] + offset[:, None]) % groups).reshape(-1)
    onehot = (target[:, None] == jnp.arange(groups, dtype=jnp.int32)[None, :]).astype(jnp.int32)
    arrival = jnp.sum((jnp.cumsum(onehot, axis=0) - onehot) * onehot, axis=1)
    orders = jax.vmap(lambda subkey: jax.random.permutation(subkey, GROUP_BLOCKS))(jax.random.split(order_key, groups)).astype(jnp.int32)
    numbers = (target * GROUP_BLOCKS + orders[target, arrival]).reshape(groups, GROUP_BLOCKS)
    shuffle = jax.vmap(lambda subkey: jax.random.permutation(subkey, GROUP_BLOCKS))(jax.random.split(shuffle_key, groups)).astype(jnp.int32)
    numbers = jnp.take_along_axis(numbers, shuffle, axis=1)
    return numbers.reshape(-1).astype(jnp.int32)


def steps_of(rng, dims, shards, smallest, high):
    gain = 1.0
    for dim, blocks in shards:
        steps = jax.random.uniform(jax.random.fold_in(jax.random.fold_in(rng, 6), dim), (blocks,), jnp.float32, smallest / len(shards), high / len(shards))
        gain = gain * jnp.repeat(jnp.exp(steps), dims[dim] // blocks).reshape((-1,) + (1,) * (len(dims) - 1 - dim))
    return gain


def centred(key, dims, deviation, most, cuts=(), held_as=jnp.bfloat16):
    level = steps_of(key, dims, cuts, -0.22, 0.18) if cuts else 1.0
    array = jax.random.normal(key, dims, jnp.float32) * deviation * level
    return jnp.minimum(jnp.maximum(array, -most), most).astype(held_as)


def setup_inputs(seed: int = 0) -> dict:
    streams_of = jax.random.split(jax.random.key(seed), 10)
    return {
        "hidden": centred(streams_of[0], (ROWS, D), 1.0, 6.0, ((0, 16),)),
        "norm_gain": jnp.clip(1.0 + 0.18 * jax.random.normal(streams_of[1], (D,), jnp.float32), 0.099609375, 1.8984375).astype(jnp.bfloat16),
        "query_weight": centred(streams_of[2], (D, QCOLS), D ** -0.5, 0.046875, ((0, 16), (1, 8))),
        "keyval_weight": centred(streams_of[3], (D, KV_HEADS, 2 * HEAD_DIM), D ** -0.5, 0.046875, ((0, 16), (1, 8))),
        "output_weight": centred(streams_of[4], (QCOLS, D), QCOLS ** -0.5, 0.046875, ((0, 8), (1, 16))),
        "kv_cache": draw_kv_cache(jax.random.fold_in(streams_of[9], 71), 0),
        "cache_lengths": draw_cache_lengths(jax.random.fold_in(streams_of[9], 71), 0),
        "next_source": centred(streams_of[7], (NBLK, BLOCK_ROWS, QCOLS), D ** -0.5, 0.046875, ((0, 128),)),
        "block_ids": draw_block_ids(jax.random.fold_in(streams_of[9], 71), 0),
    }


def attend(queries, new_keyval, kv_cache, cache_lengths):
    rows, groups, length, twice = kv_cache.shape
    head_dim = twice // 2
    score_scale = head_dim ** (-0.5)
    query_heads = queries.astype(jnp.float32).reshape(rows, groups, -1, head_dim)
    cache_float = kv_cache.astype(jnp.float32)
    fresh = new_keyval.astype(jnp.float32)
    scores = jnp.einsum('rjhd,rjpd->rjhp', query_heads, cache_float[..., :head_dim]) * score_scale
    visible = jnp.arange(length)[None, :] < cache_lengths[:, None]
    scores = jnp.where(visible[:, None, None, :], scores, -jnp.inf)
    self_score = jnp.einsum('rjhd,rjd->rjh', query_heads, fresh[..., :head_dim]) * score_scale
    highest = jnp.maximum(lax.optimization_barrier(jnp.max(scores, axis=-1)), self_score)
    expo = jnp.exp(scores - highest[..., None])
    self_expo = jnp.exp(self_score - highest)
    denominator = lax.optimization_barrier(jnp.sum(expo, axis=-1)) + self_expo
    weights = (expo / denominator[..., None]).astype(jnp.bfloat16)
    self_weight = (self_expo / denominator).astype(jnp.bfloat16)
    summed = jnp.einsum('rjhp,rjpd->rjhd', weights.astype(jnp.float32), cache_float[..., head_dim:])
    summed = summed + self_weight.astype(jnp.float32)[..., None] * fresh[:, :, None, head_dim:]
    return summed.astype(jnp.bfloat16).reshape(rows, -1)

def reference(hidden, norm_gain, query_weight, keyval_weight, output_weight, kv_cache, cache_lengths, next_source, block_ids):
    stream = hidden.astype(jnp.float32)
    meansq = lax.optimization_barrier(jnp.mean(stream * stream, axis=-1, keepdims=True))
    normed = (stream * jax.lax.rsqrt(meansq + 1e-05) * norm_gain.astype(jnp.float32)).astype(jnp.bfloat16)
    queries = jnp.dot(normed, query_weight, preferred_element_type=jnp.float32).astype(jnp.bfloat16)
    flat_kv = keyval_weight.reshape(keyval_weight.shape[0], -1)
    new_keyval = jnp.dot(normed, flat_kv, preferred_element_type=jnp.float32).astype(jnp.bfloat16)
    new_keyval = new_keyval.reshape(hidden.shape[0], KV_HEADS, 2 * HEAD_DIM)
    heads_out = attend(queries, new_keyval, kv_cache, cache_lengths)
    attention = jnp.dot(heads_out, output_weight, preferred_element_type=jnp.float32).astype(jnp.bfloat16)
    mixed = (stream + attention.astype(jnp.float32)).astype(jnp.bfloat16)
    placed = jnp.zeros((NBLK, BLOCK_ROWS, QCOLS), jnp.bfloat16).at[block_ids].set(next_source)
    return (mixed, placed.reshape(D, QCOLS))
```

```python
import functools

import jax
import jax.numpy as jnp
from jax import lax
from jax.experimental import pallas as pl
from jax.experimental.pallas import tpu as pltpu
from jax.sharding import PartitionSpec as P

ANY = pl.BlockSpec(memory_space=pl.ANY)


def scatter_kernel(ids_ref, src_ref, dst_ref, sem):
    count = src_ref.shape[0]

    @pl.loop(0, count)
    def _(b):
        pltpu.make_async_copy(src_ref.at[b], dst_ref.at[ids_ref[b]], sem).start()

    pltpu.make_async_copy(src_ref, dst_ref, sem).wait()


def scatter_slabs(ids, slabs):
    return pl.pallas_call(
        scatter_kernel,
        out_shape=jax.ShapeDtypeStruct(slabs.shape, slabs.dtype),
        in_specs=[pl.BlockSpec(memory_space=pltpu.SMEM), ANY],
        out_specs=ANY,
        scratch_shapes=[pltpu.SemaphoreType.DMA],
        cost_estimate=pl.CostEstimate(
            flops=0, bytes_accessed=2 * slabs.size * 2, transcendentals=0
        ),
        name="scatter_slabs",
    )(ids, slabs)


def swap_kernel(src_ref, dst_ref, sem):
    for m in range(src_ref.shape[0]):
        pltpu.make_async_copy(src_ref.at[m], dst_ref.at[:, m], sem).start()
    pltpu.make_async_copy(src_ref, src_ref, sem).wait()


def swap_leading(src):
    m, g, r, c = src.shape
    return pl.pallas_call(
        swap_kernel,
        out_shape=jax.ShapeDtypeStruct((g, m, r, c), src.dtype),
        in_specs=[ANY],
        out_specs=ANY,
        scratch_shapes=[pltpu.SemaphoreType.DMA],
        cost_estimate=pl.CostEstimate(flops=0, bytes_accessed=2 * src.size * 2, transcendentals=0),
        name="swap_leading",
    )(src)


def tile_kernel(src_ref, dst_ref, sem):
    tiles, width = dst_ref.shape[1], dst_ref.shape[3]
    for t in range(tiles):
        pltpu.make_async_copy(
            src_ref.at[:, :, pl.ds(t * width, width)], dst_ref.at[:, t], sem
        ).start()
    pltpu.make_async_copy(dst_ref, dst_ref, sem).wait()


def cut_tiles(src, tiles):
    m, r, c = src.shape
    return pl.pallas_call(
        tile_kernel,
        out_shape=jax.ShapeDtypeStruct((m, tiles, r, c // tiles), src.dtype),
        in_specs=[ANY],
        out_specs=ANY,
        scratch_shapes=[pltpu.SemaphoreType.DMA],
        cost_estimate=pl.CostEstimate(flops=0, bytes_accessed=2 * src.size * 2, transcendentals=0),
        name="cut_tiles",
    )(src)


def attend(queries, new_keyval, kv_cache, cache_lengths):
    rows, groups, length, twice = kv_cache.shape
    head_dim = twice // 2
    score_scale = head_dim ** (-0.5)
    query_heads = queries.reshape(rows, groups, -1, head_dim)
    scores = (
        jnp.einsum(
            "rjhd,rjpd->rjhp",
            query_heads,
            kv_cache[..., :head_dim],
            preferred_element_type=jnp.float32,
        )
        * score_scale
    )
    visible = jnp.arange(length)[None, :] < cache_lengths[:, None]
    scores = jnp.where(visible[:, None, None, :], scores, -jnp.inf)
    self_score = (
        jnp.einsum(
            "rjhd,rjd->rjh",
            query_heads,
            new_keyval[..., :head_dim],
            preferred_element_type=jnp.float32,
        )
        * score_scale
    )
    highest = jnp.maximum(jnp.max(scores, axis=-1), self_score)
    expo = jnp.exp(scores - highest[..., None])
    self_expo = jnp.exp(self_score - highest)
    denominator = jnp.sum(expo, axis=-1) + self_expo
    weights = (expo / denominator[..., None]).astype(jnp.bfloat16)
    self_weight = (self_expo / denominator).astype(jnp.bfloat16)
    summed = jnp.einsum(
        "rjhp,rjpd->rjhd", weights, kv_cache[..., head_dim:], preferred_element_type=jnp.float32
    )
    summed = summed + self_weight.astype(jnp.float32)[..., None] * new_keyval[
        :, :, None, head_dim:
    ].astype(jnp.float32)
    return summed.astype(jnp.bfloat16).reshape(rows, -1)


def exchange(x, axes):
    return lax.all_to_all(x, axes, split_axis=0, concat_axis=0, tiled=True)


def on_device(
    hidden,
    norm_gain,
    query_weight,
    keyval_weight,
    output_weight,
    kv_cache,
    cache_lengths,
    next_source,
    block_ids,
):
    barrier = lax.optimization_barrier
    dp, tensor = lax.axis_size("dp"), lax.axis_size("tensor")
    rows, width = hidden.shape
    depth = width // dp
    group = block_ids.shape[0]
    query_cols = query_weight.shape[1]

    stream = hidden.astype(jnp.float32)
    meansq = jnp.mean(stream * stream, axis=-1, keepdims=True)
    normed = (stream * lax.rsqrt(meansq + 1e-05) * norm_gain.astype(jnp.float32)).astype(
        jnp.bfloat16
    )
    lanes = jnp.broadcast_to(block_ids.astype(jnp.bfloat16)[None, :, None], (dp, group, 128))
    outbound = jnp.concatenate(
        [normed.reshape(rows, dp, depth).transpose(1, 0, 2), lanes], axis=2
    )
    arrived = exchange(outbound, "dp")
    pieces = arrived[:, :, :depth].reshape(dp * rows, depth)
    ids = arrived[:, :, depth].reshape(dp * group).astype(jnp.int32)

    block_rows = next_source.shape[1]
    piece_rows = block_rows // dp
    slabs = cut_tiles(next_source.reshape(dp, piece_rows, -1), tensor)
    tile_cols = slabs.shape[3]
    slabs = slabs.reshape(dp * tensor, piece_rows, tile_cols)
    slabs, pieces, ids = barrier((slabs, pieces, ids))
    spread = exchange(slabs, ("dp", "tensor"))

    flat_kv = keyval_weight.reshape(keyval_weight.shape[0], -1)
    partial = jnp.concatenate(
        [
            jnp.dot(pieces, query_weight, preferred_element_type=jnp.float32).astype(jnp.bfloat16),
            jnp.dot(pieces, flat_kv, preferred_element_type=jnp.float32).astype(jnp.bfloat16),
        ],
        axis=1,
    )
    partial, spread = barrier((partial, spread))
    terms = exchange(partial.reshape(dp, rows, -1), "dp")
    projected = jnp.sum(terms.astype(jnp.float32), axis=0).astype(jnp.bfloat16)

    sorted_slabs = scatter_slabs(ids, spread)
    sorted_slabs, projected = barrier((sorted_slabs, projected))
    incoming = exchange(sorted_slabs, "dp")

    queries = projected[:, :query_cols]
    new_keyval = projected[:, query_cols:].reshape(
        rows, keyval_weight.shape[1], keyval_weight.shape[2]
    )
    heads_out = attend(queries, new_keyval, kv_cache, cache_lengths)
    heads_out, incoming = barrier((heads_out, incoming))

    placed = swap_leading(incoming.reshape(dp, group, piece_rows, tile_cols))
    next_weight = placed.reshape(group * block_rows, tile_cols)

    all_heads = exchange(jnp.broadcast_to(heads_out[None], (dp,) + heads_out.shape), "dp")
    partial_out = jnp.dot(
        all_heads.reshape(dp * rows, -1), output_weight, preferred_element_type=jnp.float32
    ).astype(jnp.bfloat16)
    chunk = partial_out.shape[1] // tensor
    outbound = partial_out.reshape(dp, rows, tensor, chunk).transpose(0, 2, 1, 3)
    terms = exchange(outbound.reshape(dp * tensor, rows, chunk), ("dp", "tensor"))
    summed = jnp.sum(
        terms.reshape(dp, tensor, rows, chunk).astype(jnp.float32), axis=1
    ).astype(jnp.bfloat16)
    chunks = exchange(jnp.broadcast_to(summed[None], (tensor,) + summed.shape), "tensor")
    attention = (
        chunks.reshape(tensor, dp, rows, chunk).transpose(2, 1, 0, 3).reshape(rows, width)
    )
    mixed = (stream + attention.astype(jnp.float32)).astype(jnp.bfloat16)
    return (mixed, next_weight)


def solution(mesh):
    return jax.shard_map(
        on_device,
        mesh=mesh,
        in_specs=(
            P("dp", None),
            P(),
            P("dp", "tensor"),
            P("dp", "tensor", None),
            P("tensor", "dp"),
            P("dp", "tensor", None, None),
            P("dp"),
            P(("dp", "tensor"), None, None),
            P("dp"),
        ),
        out_specs=(P("dp", None), P("dp", "tensor")),
        check_vma=False,
    )
```

```python
import jax
import jax.numpy as jnp
from jax import lax
from jax.experimental import pallas as pl
from jax.experimental.pallas import tpu as pltpu
from jax.sharding import PartitionSpec as P

ANY = pl.BlockSpec(memory_space=pl.ANY)
VMEM = pl.BlockSpec(memory_space=pltpu.VMEM)


def pick_kernel(table_ref, src_ref, *out_refs):
    group = out_refs[0].shape[0]
    for j, out_ref in enumerate(out_refs):

        @pl.loop(0, group)
        def _(g):
            out_ref[g] = src_ref[table_ref[j * group + g]]


def pick_slabs(table, slabs, parts):
    group = table.shape[0] // parts
    part = jax.ShapeDtypeStruct((group,) + slabs.shape[1:], slabs.dtype)
    return pl.pallas_call(
        pick_kernel,
        out_shape=[part] * parts,
        in_specs=[pl.BlockSpec(memory_space=pltpu.SMEM), VMEM],
        out_specs=[VMEM] * parts,
        compiler_params=pltpu.CompilerParams(vmem_limit_bytes=32 << 20),
        cost_estimate=pl.CostEstimate(
            flops=0, bytes_accessed=2 * slabs.size * 2, transcendentals=0
        ),
        name="pick_slabs",
    )(table, slabs)


def place_kernel(owner_ref, *refs):
    *refs, dst_ref, sem = refs
    part_refs = [ref for ref in refs if ref.shape != dst_ref.shape]
    copies = [
        pltpu.make_async_copy(part_ref, dst_ref.at[:, owner_ref[j]], sem.at[j])
        for j, part_ref in enumerate(part_refs)
    ]
    for copy in copies:
        copy.start()
    for copy in copies:
        copy.wait()


def place_parts(owners, parts, count, into=None):
    group, r, c = parts[0].shape
    held = [] if into is None else [into]
    return pl.pallas_call(
        place_kernel,
        out_shape=jax.ShapeDtypeStruct((group, count, r, c), parts[0].dtype),
        in_specs=[pl.BlockSpec(memory_space=pltpu.SMEM)] + [VMEM] * len(parts) + [ANY] * len(held),
        out_specs=ANY,
        input_output_aliases={1 + len(parts): 0} if held else {},
        scratch_shapes=[pltpu.SemaphoreType.DMA((len(parts),))],
        compiler_params=pltpu.CompilerParams(vmem_limit_bytes=16 << 20),
        cost_estimate=pl.CostEstimate(
            flops=0, bytes_accessed=4 * len(parts) * parts[0].size, transcendentals=0
        ),
        name="place_parts",
    )(owners, *parts, *held)


ROUNDS = (
    ((0, 1, 0), (1, 3, 1), (1, 2, 0), (0, 0, 1)),
    ((0, 1, 1), (1, 3, 0), (0, 2, 1), (1, 0, 0)),
    ((1, 1, 0), (0, 3, 1), (0, 2, 0), (1, 0, 1)),
    ((1, 1, 1), (0, 3, 0), (1, 2, 1)),
)
STEPS = ((0, 0, 0),) + tuple(step for steps in ROUNDS for step in steps)


def shifted(index, step, sign):
    y_lo, x, core = index // 8, index // 2 % 4, index % 2
    return ((y_lo + step[0]) % 2 * 4 + (x + sign * step[1]) % 4) * 2 + (core + step[2]) % 2


def send(part, step):
    return lax.ppermute(part, "dp", [(s, shifted(s, step, 1)) for s in range(16)])


def attend(queries, new_keyval, kv_cache, cache_lengths):
    rows, groups, length, twice = kv_cache.shape
    head_dim = twice // 2
    score_scale = head_dim ** (-0.5)
    query_heads = queries.reshape(rows, groups, -1, head_dim)
    scores = (
        jnp.einsum(
            "rjhd,rjpd->rjhp",
            query_heads,
            kv_cache[..., :head_dim],
            preferred_element_type=jnp.float32,
        )
        * score_scale
    )
    visible = jnp.arange(length)[None, :] < cache_lengths[:, None]
    scores = jnp.where(visible[:, None, None, :], scores, -jnp.inf)
    self_score = (
        jnp.einsum(
            "rjhd,rjd->rjh",
            query_heads,
            new_keyval[..., :head_dim],
            preferred_element_type=jnp.float32,
        )
        * score_scale
    )
    highest = jnp.maximum(jnp.max(scores, axis=-1), self_score)
    expo = jnp.exp(scores - highest[..., None])
    self_expo = jnp.exp(self_score - highest)
    denominator = jnp.sum(expo, axis=-1) + self_expo
    weights = (expo / denominator[..., None]).astype(jnp.bfloat16)
    self_weight = (self_expo / denominator).astype(jnp.bfloat16)
    summed = jnp.einsum(
        "rjhp,rjpd->rjhd", weights, kv_cache[..., head_dim:], preferred_element_type=jnp.float32
    )
    summed = summed + self_weight.astype(jnp.float32)[..., None] * new_keyval[
        :, :, None, head_dim:
    ].astype(jnp.float32)
    return summed.astype(jnp.bfloat16).reshape(rows, -1)


def exchange(x, axes):
    return lax.all_to_all(x, axes, split_axis=0, concat_axis=0, tiled=True)


def on_device(
    hidden,
    norm_gain,
    query_weight,
    keyval_weight,
    output_weight,
    kv_cache,
    cache_lengths,
    next_source,
    block_ids,
):
    barrier = lax.optimization_barrier
    dp, tensor = lax.axis_size("dp"), lax.axis_size("tensor")
    rows, width = hidden.shape
    depth = width // dp
    group = block_ids.shape[0]
    query_cols = query_weight.shape[1]

    mine = lax.axis_index("dp")
    lanes = jnp.broadcast_to(block_ids.astype(jnp.bfloat16)[None, :, None], (dp, group, 128))
    outbound = jnp.concatenate(
        [hidden.reshape(rows, dp, depth).transpose(1, 0, 2), lanes], axis=2
    )
    arrived = exchange(outbound, "dp")

    block_rows = next_source.shape[1]
    piece_rows = block_rows // dp
    tile_cols = next_source.shape[2] // tensor
    slabs = next_source.reshape(dp, piece_rows, tensor, tile_cols).transpose(0, 2, 1, 3)
    slabs, arrived = barrier((slabs.reshape(dp * tensor, piece_rows, tile_cols), arrived))
    spread = exchange(slabs, ("dp", "tensor"))

    stream = hidden.astype(jnp.float32)
    meansq = jnp.mean(stream * stream, axis=-1, keepdims=True)
    row_scale = lax.rsqrt(meansq + 1e-05)

    gain = lax.dynamic_slice(norm_gain, (mine * depth,), (depth,))
    pieces = (
        arrived[:, :, :depth].reshape(dp * rows, depth).astype(jnp.float32)
        * gain.astype(jnp.float32)
    ).astype(jnp.bfloat16)
    flat_kv = keyval_weight.reshape(keyval_weight.shape[0], -1)
    partial = jnp.concatenate(
        [
            jnp.dot(pieces, query_weight, preferred_element_type=jnp.float32).astype(jnp.bfloat16),
            jnp.dot(pieces, flat_kv, preferred_element_type=jnp.float32).astype(jnp.bfloat16),
        ],
        axis=1,
    )

    ids = arrived[:, :, depth].reshape(dp * group).astype(jnp.int32)
    targets = jnp.stack([shifted(mine, step, 1) for step in STEPS])
    wanted = (targets[:, None] * group + jnp.arange(group, dtype=jnp.int32)[None, :]).reshape(-1)
    table = jnp.sum(
        jnp.where(
            ids[None, :] == wanted[:, None],
            jnp.arange(dp * group, dtype=jnp.int32)[None, :],
            0,
        ),
        axis=1,
    )
    owners = jnp.stack([shifted(mine, step, -1) for step in STEPS])
    partial, row_scale, table, spread = barrier((partial, row_scale, table, spread))
    terms = exchange(partial.reshape(dp, rows, -1), "dp")
    bounds = [0, 1 + len(ROUNDS[0])]
    for steps in ROUNDS[1:]:
        bounds.append(bounds[-1] + len(steps))
    picked = [
        pick_slabs(table[first * group : last * group], spread, last - first)
        for first, last in zip(bounds[:-1], bounds[1:])
    ]

    def start_round(number, anchor):
        anchor, *ready = barrier((anchor, *picked[number]))
        return anchor, [send(part, step) for part, step in zip(ready, ROUNDS[number])]

    kept, *ready = picked[0]
    landed = [[kept] + [send(part, step) for part, step in zip(ready, ROUNDS[0])]]
    projected = (jnp.sum(terms.astype(jnp.float32), axis=0) * row_scale).astype(jnp.bfloat16)
    queries = projected[:, :query_cols]
    new_keyval = projected[:, query_cols:].reshape(
        rows, keyval_weight.shape[1], keyval_weight.shape[2]
    )
    heads_out = attend(queries, new_keyval, kv_cache, cache_lengths)

    heads_out, results = start_round(1, heads_out)
    landed.append(results)
    all_heads = exchange(jnp.broadcast_to(heads_out[None], (dp,) + heads_out.shape), "dp")
    partial_out = jnp.dot(
        all_heads.reshape(dp * rows, -1), output_weight, preferred_element_type=jnp.float32
    ).astype(jnp.bfloat16)
    chunk = partial_out.shape[1] // tensor
    outbound = partial_out.reshape(dp, rows, tensor, chunk).transpose(0, 2, 1, 3)
    outbound = outbound.reshape(dp * tensor, rows, chunk)

    outbound, results = start_round(2, outbound)
    landed.append(results)
    terms = exchange(outbound, ("dp", "tensor"))
    summed = jnp.sum(
        terms.reshape(dp, tensor, rows, chunk).astype(jnp.float32), axis=1
    ).astype(jnp.bfloat16)

    first_rows = [owners[first:last] for first, last in zip(bounds[:-1], bounds[1:])]
    placed = place_parts(first_rows[0], landed[0], dp)
    placed = place_parts(first_rows[1], landed[1], dp, placed)
    summed, placed = barrier((summed, placed))
    summed, results = start_round(3, summed)
    landed.append(results)
    chunks = exchange(jnp.broadcast_to(summed[None], (tensor,) + summed.shape), "tensor")
    attention = (
        chunks.reshape(tensor, dp, rows, chunk).transpose(2, 1, 0, 3).reshape(rows, width)
    )
    mixed = (stream + attention.astype(jnp.float32)).astype(jnp.bfloat16)

    placed = place_parts(first_rows[2], landed[2], dp, placed)
    placed = place_parts(first_rows[3], landed[3], dp, placed)
    next_weight = placed.reshape(group * block_rows, tile_cols)
    return (mixed, next_weight)


def solution(mesh):
    return jax.shard_map(
        on_device,
        mesh=mesh,
        in_specs=(
            P("dp", None),
            P(),
            P("dp", "tensor"),
            P("dp", "tensor", None),
            P("tensor", "dp"),
            P("dp", "tensor", None, None),
            P("dp"),
            P(("dp", "tensor"), None, None),
            P("dp"),
        ),
        out_specs=(P("dp", None), P("dp", "tensor")),
        check_vma=False,
    )
```

```python
import jax
import jax.numpy as jnp
from jax import lax
from jax.experimental import pallas as pl
from jax.experimental.pallas import tpu as pltpu
from jax.sharding import PartitionSpec as P

ANY = pl.BlockSpec(memory_space=pl.ANY)
HBM = pl.BlockSpec(memory_space=pltpu.HBM)
VMEM = pl.BlockSpec(memory_space=pltpu.VMEM)
SMEM = pl.BlockSpec(memory_space=pltpu.SMEM)
LANES = 128


def cost(flops, bytes_accessed):
    return pl.CostEstimate(flops=flops, bytes_accessed=bytes_accessed, transcendentals=0)


def prep_kernel(ids_ref, hidden_ref, out_ref):
    parts, rows, wide = out_ref.shape
    depth = wide - LANES
    row = lax.broadcasted_iota(jnp.int32, (rows, LANES), 0)
    numbers = jnp.zeros((rows, LANES), jnp.int32)
    for i in range(rows):
        numbers = jnp.where(row == i, ids_ref[i], numbers)
    numbers = numbers.astype(jnp.float32).astype(out_ref.dtype)
    for m in range(parts):
        out_ref[m, :, :depth] = hidden_ref[:, m * depth : (m + 1) * depth]
        out_ref[m, :, depth:] = numbers


def prepare(ids, hidden, parts):
    rows, width = hidden.shape
    return pl.pallas_call(
        prep_kernel,
        out_shape=jax.ShapeDtypeStruct((parts, rows, width // parts + LANES), hidden.dtype),
        in_specs=[SMEM, VMEM],
        out_specs=VMEM,
        cost_estimate=cost(0, 4 * hidden.size),
        name="prepare",
    )(ids, hidden)


def attend_kernel(
    lengths_ref, terms_ref, scale_ref, cache_ref, out_ref,
    query_ref, held_ref, score_ref, weight_ref, sums_ref, sems,
):
    copies, rows, query_cols = out_ref.shape
    length, head_dim = cache_ref.shape[1], cache_ref.shape[2] // 2
    heads = query_cols // head_dim
    reads = [
        pltpu.make_async_copy(cache_ref.at[r], held_ref.at[r], sems.at[r]) for r in range(rows)
    ]
    for read in reads:
        read.start()
    total = terms_ref[0].astype(jnp.float32)
    for s in range(1, terms_ref.shape[0]):
        total = total + terms_ref[s].astype(jnp.float32)
    total = (total * scale_ref[...]).astype(jnp.bfloat16).astype(jnp.float32)
    for h in range(heads):
        query_ref[:, h, :] = total[:, h * head_dim : (h + 1) * head_dim]
    new_key = total[:, query_cols : query_cols + head_dim]
    new_value = total[:, query_cols + head_dim :]
    position = lax.broadcasted_iota(jnp.int32, (heads, length), 1)
    score_scale = head_dim ** (-0.5)
    for r in range(rows):
        reads[r].wait()
        scores = lax.dot_general(
            query_ref[r].astype(jnp.bfloat16),
            held_ref[r, :, :head_dim],
            (((1,), (1,)), ((), ())),
            preferred_element_type=jnp.float32,
        )
        score_ref[r] = jnp.where(position < lengths_ref[r], scores * score_scale, -jnp.inf)
    self_score = jnp.sum(query_ref[...] * new_key[:, None, :], axis=2, keepdims=True) * score_scale
    scores = score_ref[...]
    highest = jnp.maximum(jnp.max(scores, axis=2, keepdims=True), self_score)
    expo = jnp.exp(scores - highest)
    self_expo = jnp.exp(self_score - highest)
    denominator = jnp.sum(expo, axis=2, keepdims=True) + self_expo
    weight_ref[...] = (expo / denominator).astype(jnp.bfloat16)
    self_weight = (self_expo / denominator).astype(jnp.bfloat16).astype(jnp.float32)
    sums_ref[...] = self_weight * new_value[:, None, :]
    for r in range(rows):
        sums_ref[r] += jnp.dot(
            weight_ref[r], held_ref[r, :, head_dim:], preferred_element_type=jnp.float32
        )
    for h in range(heads):
        head = sums_ref[:, h, :].astype(out_ref.dtype)
        for copy in range(copies):
            out_ref[copy, :, h * head_dim : (h + 1) * head_dim] = head


def attend(lengths, terms, row_scale, cache):
    copies, rows, cols = terms.shape
    _, length, twice = cache.shape
    head_dim = twice // 2
    query_cols = cols - twice
    heads = query_cols // head_dim
    return pl.pallas_call(
        attend_kernel,
        out_shape=jax.ShapeDtypeStruct((copies, rows, query_cols), jnp.bfloat16),
        in_specs=[SMEM, VMEM, VMEM, HBM],
        out_specs=VMEM,
        scratch_shapes=[
            pltpu.VMEM((rows, heads, head_dim), jnp.float32),
            pltpu.VMEM(cache.shape, cache.dtype),
            pltpu.VMEM((rows, heads, length), jnp.float32),
            pltpu.VMEM((rows, heads, length), jnp.bfloat16),
            pltpu.VMEM((rows, heads, head_dim), jnp.float32),
            pltpu.SemaphoreType.DMA((rows,)),
        ],
        compiler_params=pltpu.CompilerParams(vmem_limit_bytes=60 << 20),
        cost_estimate=cost(4 * cache.size * heads, 2 * cache.size),
        name="attend",
    )(lengths, terms, row_scale, cache)


def output_kernel(heads_ref, weight_ref, out_ref, held_ref, total_ref, sems):
    parts, chunks, rows, chunk = out_ref.shape
    count, depth, cols = held_ref.shape
    reads = [
        pltpu.make_async_copy(
            weight_ref.at[pl.ds(k * depth, depth)], held_ref.at[k], sems.at[k]
        )
        for k in range(count)
    ]
    for read in reads:
        read.start()
    step = 2 * chunk
    for k, read in enumerate(reads):
        read.wait()
        heads = heads_ref[:, k * depth : (k + 1) * depth]
        for j in range(0, cols, step):
            product = jnp.dot(
                heads, held_ref[k, :, j : j + step], preferred_element_type=jnp.float32
            )
            if k:
                product = total_ref[:, j : j + step] + product
            if k < count - 1:
                total_ref[:, j : j + step] = product
                continue
            for i in range(2):
                tile = product[:, i * chunk : (i + 1) * chunk].reshape(parts, rows, chunk)
                out_ref[:, j // chunk + i] = tile.astype(out_ref.dtype)


def project_out(heads, weight, parts, chunks):
    rows, cols = heads.shape[0], weight.shape[1]
    steps = 4
    return pl.pallas_call(
        output_kernel,
        out_shape=jax.ShapeDtypeStruct(
            (parts, chunks, rows // parts, cols // chunks), jnp.bfloat16
        ),
        in_specs=[VMEM, HBM],
        out_specs=VMEM,
        scratch_shapes=[
            pltpu.VMEM((steps, weight.shape[0] // steps, cols), weight.dtype),
            pltpu.VMEM((rows, cols), jnp.float32),
            pltpu.SemaphoreType.DMA((steps,)),
        ],
        compiler_params=pltpu.CompilerParams(vmem_limit_bytes=60 << 20),
        cost_estimate=cost(2 * rows * weight.size, 2 * weight.size),
        name="project_out",
    )(heads, weight)


def pick_kernel(table_ref, src_ref, *refs):
    *out_refs, sem = refs
    count, _, width = out_refs[0].shape
    for j, out_ref in enumerate(out_refs):
        for i in range(count):
            pltpu.make_async_copy(
                src_ref.at[table_ref[j * count + i], :, pl.ds(0, width)], out_ref.at[i], sem.at[j]
            ).start()
    for j, out_ref in enumerate(out_refs):
        pltpu.make_async_copy(out_ref, out_ref, sem.at[j]).wait()


def pick_slabs(table, slabs, parts):
    count = table.shape[0] // parts
    shape = (count, slabs.shape[1], slabs.shape[2])
    return pl.pallas_call(
        pick_kernel,
        out_shape=[jax.ShapeDtypeStruct(shape, slabs.dtype)] * parts,
        in_specs=[SMEM, HBM],
        out_specs=[VMEM] * parts,
        scratch_shapes=[pltpu.SemaphoreType.DMA((parts,))],
        compiler_params=pltpu.CompilerParams(vmem_limit_bytes=16 << 20),
        cost_estimate=cost(0, 4 * parts * count * slabs[0].size),
        name="pick_slabs",
    )(table, slabs)


def place_kernel(owner_ref, *refs):
    *refs, dst_ref, sem = refs
    part_refs = [ref for ref in refs if ref.shape != dst_ref.shape]
    copies = [
        pltpu.make_async_copy(part_ref, dst_ref.at[:, owner_ref[j]], sem.at[j])
        for j, part_ref in enumerate(part_refs)
    ]
    for copy in copies:
        copy.start()
    for copy in copies:
        copy.wait()


def place_parts(owners, parts, count, into=None):
    group, r, c = parts[0].shape
    held = [] if into is None else [into]
    return pl.pallas_call(
        place_kernel,
        out_shape=jax.ShapeDtypeStruct((group, count, r, c), parts[0].dtype),
        in_specs=[SMEM] + [VMEM] * len(parts) + [ANY] * len(held),
        out_specs=ANY,
        input_output_aliases={1 + len(parts): 0} if held else {},
        scratch_shapes=[pltpu.SemaphoreType.DMA((len(parts),))],
        compiler_params=pltpu.CompilerParams(vmem_limit_bytes=16 << 20),
        cost_estimate=pl.CostEstimate(
            flops=0, bytes_accessed=4 * len(parts) * parts[0].size, transcendentals=0
        ),
        name="place_parts",
    )(owners, *parts, *held)


ROUNDS = (
    ((0, 1, 0), (1, 3, 1)),
    ((0, 2, 0), (1, 0, 0), (1, 1, 0), (0, 3, 0), (0, 2, 1)),
    ((1, 0, 1), (0, 1, 1), (1, 3, 0), (1, 1, 1)),
    ((0, 3, 1), (1, 2, 0), (0, 0, 1), (1, 2, 1)),
)
STEPS = ((0, 0, 0),) + tuple(step for steps in ROUNDS for step in steps)
FENCES = {'heads': 3}
EARLY = 8


def shifted(index, step, sign):
    y_lo, x, core = index // 8, index // 2 % 4, index % 2
    return ((y_lo + step[0]) % 2 * 4 + (x + sign * step[1]) % 4) * 2 + (core + step[2]) % 2


def send(part, step):
    return lax.ppermute(part, "dp", [(s, shifted(s, step, 1)) for s in range(16)])


def sum_kernel(terms_ref, out_ref):
    for m in range(terms_ref.shape[0]):
        total = terms_ref[m, 0].astype(jnp.float32)
        for t in range(1, terms_ref.shape[1]):
            total = total + terms_ref[m, t].astype(jnp.float32)
        total = total.astype(out_ref.dtype)
        for copy in range(out_ref.shape[0]):
            out_ref[copy, m] = total


def sum_over_tensor(terms):
    dp, tensor, rows, chunk = terms.shape
    return pl.pallas_call(
        sum_kernel,
        out_shape=jax.ShapeDtypeStruct((tensor, dp, rows, chunk), terms.dtype),
        in_specs=[VMEM],
        out_specs=VMEM,
        cost_estimate=cost(terms.size, 4 * terms.size),
        name="sum_over_tensor",
    )(terms)


def mix_kernel(hidden_ref, chunks_ref, out_ref):
    tensor, dp, _, chunk = chunks_ref.shape
    for m in range(dp):
        for t in range(tensor):
            columns = slice((m * tensor + t) * chunk, (m * tensor + t + 1) * chunk)
            out_ref[:, columns] = (
                hidden_ref[:, columns].astype(jnp.float32)
                + chunks_ref[t, m].astype(jnp.float32)
            ).astype(out_ref.dtype)


def mix(hidden, chunks):
    return pl.pallas_call(
        mix_kernel,
        out_shape=jax.ShapeDtypeStruct(hidden.shape, hidden.dtype),
        in_specs=[VMEM, VMEM],
        out_specs=VMEM,
        cost_estimate=cost(hidden.size, 6 * hidden.size),
        name="mix",
    )(hidden, chunks)


def exchange(x, axes):
    return lax.all_to_all(x, axes, split_axis=0, concat_axis=0, tiled=True)


def on_device(
    hidden,
    norm_gain,
    query_weight,
    keyval_weight,
    output_weight,
    kv_cache,
    cache_lengths,
    next_source,
    block_ids,
):
    barrier = lax.optimization_barrier
    dp, tensor = lax.axis_size("dp"), lax.axis_size("tensor")
    rows, width = hidden.shape
    depth = width // dp
    group = block_ids.shape[0]
    mine = lax.axis_index("dp")

    arrived = exchange(prepare(block_ids, hidden, dp), "dp")

    block_rows = next_source.shape[1]
    piece_rows = block_rows // dp
    tile_cols = next_source.shape[2] // tensor
    slabs = next_source.reshape(dp, piece_rows, tensor, tile_cols).transpose(0, 2, 1, 3)
    slabs, arrived = barrier((slabs.reshape(dp * tensor, piece_rows, tile_cols), arrived))
    spread = exchange(slabs, ("dp", "tensor"))

    stream = hidden.astype(jnp.float32)
    meansq = jnp.mean(stream * stream, axis=-1, keepdims=True)
    row_scale = lax.rsqrt(meansq + 1e-05)
    gain = lax.dynamic_slice(norm_gain, (mine * depth,), (depth,))
    pieces = (
        arrived[:, :, :depth].reshape(dp * rows, depth).astype(jnp.float32)
        * gain.astype(jnp.float32)
    ).astype(jnp.bfloat16)
    flat_kv = keyval_weight.reshape(keyval_weight.shape[0], -1)
    partial = jnp.concatenate(
        [
            jnp.dot(pieces, query_weight, preferred_element_type=jnp.float32).astype(jnp.bfloat16),
            jnp.dot(pieces, flat_kv, preferred_element_type=jnp.float32).astype(jnp.bfloat16),
        ],
        axis=1,
    )
    cache = kv_cache.reshape(rows, kv_cache.shape[2], kv_cache.shape[3])
    ids = arrived[:, :, depth].reshape(dp * group).astype(jnp.int32)
    targets = jnp.stack([shifted(mine, step, 1) for step in STEPS])
    wanted = (targets[:, None] * group + jnp.arange(group, dtype=jnp.int32)[None, :]).reshape(-1)
    table = jnp.sum(
        jnp.where(
            ids[None, :] == wanted[:, None],
            jnp.arange(dp * group, dtype=jnp.int32)[None, :],
            0,
        ),
        axis=1,
    )
    owners = jnp.stack([shifted(mine, step, -1) for step in STEPS])
    partial, row_scale, table, owners, spread = barrier(
        (partial, row_scale, table, owners, spread)
    )

    terms = exchange(partial.reshape(dp, rows, -1), "dp")

    bounds = [0, 1 + len(ROUNDS[0])]
    for steps in ROUNDS[1:]:
        bounds.append(bounds[-1] + len(steps))
    tables = [table[group * i : group * j] for i, j in zip(bounds[:-1], bounds[1:])]
    kept, *ready = pick_slabs(tables[0], spread, bounds[1])
    landed = [kept] + [send(part, step) for part, step in zip(ready, ROUNDS[0])]

    def start_round(number, anchor):
        count = len(ROUNDS[number])
        anchor, *ready = barrier((anchor, *pick_slabs(tables[number], spread, count)))
        landed.extend(send(part, step) for part, step in zip(ready, ROUNDS[number]))
        return anchor

    def fence(name, anchor):
        count = FENCES.get(name, 0)
        anchor, *done = barrier((anchor, *landed[:count]))
        landed[:count] = done
        return anchor

    heads_out = attend(cache_lengths, terms, row_scale, cache)
    heads_out = fence("heads", heads_out)
    heads_out = start_round(1, heads_out)
    all_heads = exchange(heads_out, "dp")
    outbound = project_out(all_heads.reshape(dp * rows, -1), output_weight, dp, tensor)
    chunk = outbound.shape[3]
    outbound = outbound.reshape(dp * tensor, rows, chunk)
    outbound = fence("outbound", outbound)
    outbound = start_round(2, outbound)
    terms = exchange(outbound, ("dp", "tensor"))
    summed = sum_over_tensor(terms.reshape(dp, tensor, rows, chunk))
    summed = fence("summed", summed)
    placed = place_parts(owners[:EARLY], landed[:EARLY], dp)
    summed, placed = barrier((summed, placed))
    summed = start_round(3, summed)
    chunks = exchange(summed, "tensor")
    mixed = mix(hidden, chunks)

    placed = place_parts(owners[EARLY:], landed[EARLY:], dp, placed)
    next_weight = placed.reshape(group * block_rows, tile_cols)
    return (mixed, next_weight)


def solution(mesh):
    return jax.shard_map(
        on_device,
        mesh=mesh,
        in_specs=(
            P("dp", None),
            P(),
            P("dp", "tensor"),
            P("dp", "tensor", None),
            P("tensor", "dp"),
            P("dp", "tensor", None, None),
            P("dp"),
            P(("dp", "tensor"), None, None),
            P("dp"),
        ),
        out_specs=(P("dp", None), P("dp", "tensor")),
        check_vma=False,
    )
```

```python
import jax
import jax.numpy as jnp
from jax import lax
from jax.experimental import pallas as pl
from jax.experimental.pallas import tpu as pltpu
from jax.sharding import PartitionSpec as P

ANY = pl.BlockSpec(memory_space=pl.ANY)
HBM = pl.BlockSpec(memory_space=pltpu.HBM)
VMEM = pl.BlockSpec(memory_space=pltpu.VMEM)
SMEM = pl.BlockSpec(memory_space=pltpu.SMEM)
LANES = 128


def cost(flops, bytes_accessed):
    return pl.CostEstimate(flops=flops, bytes_accessed=bytes_accessed, transcendentals=0)


def prep_kernel(ids_ref, hidden_ref, out_ref):
    parts, rows, wide = out_ref.shape
    depth = wide - LANES
    row = lax.broadcasted_iota(jnp.int32, (rows, LANES), 0)
    numbers = jnp.zeros((rows, LANES), jnp.int32)
    for i in range(rows):
        numbers = jnp.where(row == i, ids_ref[i], numbers)
    numbers = numbers.astype(jnp.float32).astype(out_ref.dtype)
    for m in range(parts):
        out_ref[m, :, :depth] = hidden_ref[:, m * depth : (m + 1) * depth]
        out_ref[m, :, depth:] = numbers


def prepare(ids, hidden, parts):
    rows, width = hidden.shape
    return pl.pallas_call(
        prep_kernel,
        out_shape=jax.ShapeDtypeStruct((parts, rows, width // parts + LANES), hidden.dtype),
        in_specs=[SMEM, VMEM],
        out_specs=VMEM,
        cost_estimate=cost(0, 4 * hidden.size),
        name="prepare",
    )(ids, hidden)


def attend_kernel(
    lengths_ref, terms_ref, scale_ref, cache_ref, out_ref,
    query_ref, score_ref, weight_ref, sums_ref,
):
    copies, rows, query_cols = out_ref.shape
    length, head_dim = cache_ref.shape[1], cache_ref.shape[2] // 2
    heads = query_cols // head_dim
    total = terms_ref[0].astype(jnp.float32)
    for s in range(1, terms_ref.shape[0]):
        total = total + terms_ref[s].astype(jnp.float32)
    total = (total * scale_ref[...]).astype(jnp.bfloat16).astype(jnp.float32)
    for h in range(heads):
        query_ref[:, h, :] = total[:, h * head_dim : (h + 1) * head_dim]
    new_key = total[:, query_cols : query_cols + head_dim]
    new_value = total[:, query_cols + head_dim :]
    position = lax.broadcasted_iota(jnp.int32, (heads, length), 1)
    score_scale = head_dim ** (-0.5)
    for r in range(rows):
        scores = lax.dot_general(
            query_ref[r].astype(jnp.bfloat16),
            cache_ref[r, :, :head_dim],
            (((1,), (1,)), ((), ())),
            preferred_element_type=jnp.float32,
        )
        score_ref[r] = jnp.where(position < lengths_ref[r], scores * score_scale, -jnp.inf)
    self_score = jnp.sum(query_ref[...] * new_key[:, None, :], axis=2, keepdims=True) * score_scale
    scores = score_ref[...]
    highest = jnp.maximum(jnp.max(scores, axis=2, keepdims=True), self_score)
    expo = jnp.exp(scores - highest)
    self_expo = jnp.exp(self_score - highest)
    denominator = jnp.sum(expo, axis=2, keepdims=True) + self_expo
    weight_ref[...] = (expo / denominator).astype(jnp.bfloat16)
    self_weight = (self_expo / denominator).astype(jnp.bfloat16).astype(jnp.float32)
    sums_ref[...] = self_weight * new_value[:, None, :]
    for r in range(rows):
        sums_ref[r] += jnp.dot(
            weight_ref[r], cache_ref[r, :, head_dim:], preferred_element_type=jnp.float32
        )
    for h in range(heads):
        head = sums_ref[:, h, :].astype(out_ref.dtype)
        for copy in range(copies):
            out_ref[copy, :, h * head_dim : (h + 1) * head_dim] = head


def attend(lengths, terms, row_scale, cache):
    copies, rows, cols = terms.shape
    _, length, twice = cache.shape
    head_dim = twice // 2
    query_cols = cols - twice
    heads = query_cols // head_dim
    return pl.pallas_call(
        attend_kernel,
        out_shape=jax.ShapeDtypeStruct((copies, rows, query_cols), jnp.bfloat16),
        in_specs=[SMEM, VMEM, VMEM, VMEM],
        out_specs=VMEM,
        scratch_shapes=[
            pltpu.VMEM((rows, heads, head_dim), jnp.float32),
            pltpu.VMEM((rows, heads, length), jnp.float32),
            pltpu.VMEM((rows, heads, length), jnp.bfloat16),
            pltpu.VMEM((rows, heads, head_dim), jnp.float32),
        ],
        compiler_params=pltpu.CompilerParams(vmem_limit_bytes=16 << 20),
        cost_estimate=cost(4 * cache.size * heads, 2 * cache.size),
        name="attend",
    )(lengths, terms, row_scale, cache)


def output_kernel(heads_ref, weight_ref, out_ref):
    parts, chunks, rows, chunk = out_ref.shape
    step = 2 * chunk
    for j in range(chunks // 2):
        product = jnp.dot(
            heads_ref[...],
            weight_ref[:, j * step : (j + 1) * step],
            preferred_element_type=jnp.float32,
        )
        for k in range(2):
            tile = product[:, k * chunk : (k + 1) * chunk].reshape(parts, rows, chunk)
            out_ref[:, 2 * j + k] = tile.astype(out_ref.dtype)


def project_out(heads, weight, parts, chunks):
    rows, cols = heads.shape[0], weight.shape[1]
    return pl.pallas_call(
        output_kernel,
        out_shape=jax.ShapeDtypeStruct(
            (parts, chunks, rows // parts, cols // chunks), jnp.bfloat16
        ),
        in_specs=[VMEM, VMEM],
        out_specs=VMEM,
        compiler_params=pltpu.CompilerParams(vmem_limit_bytes=16 << 20),
        cost_estimate=cost(2 * rows * weight.size, 2 * weight.size),
        name="project_out",
    )(heads, weight)


def pick_kernel(table_ref, src_ref, *refs):
    *out_refs, sem = refs
    count, _, width = out_refs[0].shape
    for j, out_ref in enumerate(out_refs):
        for i in range(count):
            pltpu.make_async_copy(
                src_ref.at[table_ref[j * count + i], :, pl.ds(0, width)], out_ref.at[i], sem.at[j]
            ).start()
    for j, out_ref in enumerate(out_refs):
        pltpu.make_async_copy(out_ref, out_ref, sem.at[j]).wait()


def pick_slabs(table, slabs, parts):
    count = table.shape[0] // parts
    shape = (count, slabs.shape[1], slabs.shape[2])
    return pl.pallas_call(
        pick_kernel,
        out_shape=[jax.ShapeDtypeStruct(shape, slabs.dtype)] * parts,
        in_specs=[SMEM, HBM],
        out_specs=[VMEM] * parts,
        scratch_shapes=[pltpu.SemaphoreType.DMA((parts,))],
        compiler_params=pltpu.CompilerParams(vmem_limit_bytes=16 << 20),
        cost_estimate=cost(0, 4 * parts * count * slabs[0].size),
        name="pick_slabs",
    )(table, slabs)


def place_kernel(owner_ref, *refs):
    *refs, dst_ref, sem = refs
    part_refs = [ref for ref in refs if ref.shape != dst_ref.shape]
    copies = [
        pltpu.make_async_copy(part_ref, dst_ref.at[:, owner_ref[j]], sem.at[j])
        for j, part_ref in enumerate(part_refs)
    ]
    for copy in copies:
        copy.start()
    for copy in copies:
        copy.wait()


def place_parts(owners, parts, count, into=None):
    group, r, c = parts[0].shape
    held = [] if into is None else [into]
    return pl.pallas_call(
        place_kernel,
        out_shape=jax.ShapeDtypeStruct((group, count, r, c), parts[0].dtype),
        in_specs=[SMEM] + [VMEM] * len(parts) + [ANY] * len(held),
        out_specs=ANY,
        input_output_aliases={1 + len(parts): 0} if held else {},
        scratch_shapes=[pltpu.SemaphoreType.DMA((len(parts),))],
        compiler_params=pltpu.CompilerParams(vmem_limit_bytes=16 << 20),
        cost_estimate=pl.CostEstimate(
            flops=0, bytes_accessed=4 * len(parts) * parts[0].size, transcendentals=0
        ),
        name="place_parts",
    )(owners, *parts, *held)


ROUNDS = (
    ((0, 1, 0), (1, 3, 1)),
    ((0, 2, 0), (1, 0, 0), (1, 1, 0), (0, 3, 0), (0, 2, 1)),
    ((1, 0, 1), (0, 1, 1), (1, 3, 0), (1, 1, 1)),
    ((0, 3, 1), (1, 2, 0), (0, 0, 1), (1, 2, 1)),
)
STEPS = ((0, 0, 0),) + tuple(step for steps in ROUNDS for step in steps)
FENCES = {'heads': 3}
EARLY = 8


def shifted(index, step, sign):
    y_lo, x, core = index // 8, index // 2 % 4, index % 2
    return ((y_lo + step[0]) % 2 * 4 + (x + sign * step[1]) % 4) * 2 + (core + step[2]) % 2


def send(part, step):
    return lax.ppermute(part, "dp", [(s, shifted(s, step, 1)) for s in range(16)])


def sum_kernel(terms_ref, out_ref):
    for m in range(terms_ref.shape[0]):
        total = terms_ref[m, 0].astype(jnp.float32)
        for t in range(1, terms_ref.shape[1]):
            total = total + terms_ref[m, t].astype(jnp.float32)
        total = total.astype(out_ref.dtype)
        for copy in range(out_ref.shape[0]):
            out_ref[copy, m] = total


def sum_over_tensor(terms):
    dp, tensor, rows, chunk = terms.shape
    return pl.pallas_call(
        sum_kernel,
        out_shape=jax.ShapeDtypeStruct((tensor, dp, rows, chunk), terms.dtype),
        in_specs=[VMEM],
        out_specs=VMEM,
        cost_estimate=cost(terms.size, 4 * terms.size),
        name="sum_over_tensor",
    )(terms)


def mix_kernel(hidden_ref, chunks_ref, out_ref):
    tensor, dp, _, chunk = chunks_ref.shape
    for m in range(dp):
        for t in range(tensor):
            columns = slice((m * tensor + t) * chunk, (m * tensor + t + 1) * chunk)
            out_ref[:, columns] = (
                hidden_ref[:, columns].astype(jnp.float32)
                + chunks_ref[t, m].astype(jnp.float32)
            ).astype(out_ref.dtype)


def mix(hidden, chunks):
    return pl.pallas_call(
        mix_kernel,
        out_shape=jax.ShapeDtypeStruct(hidden.shape, hidden.dtype),
        in_specs=[VMEM, VMEM],
        out_specs=VMEM,
        cost_estimate=cost(hidden.size, 6 * hidden.size),
        name="mix",
    )(hidden, chunks)


def exchange(x, axes):
    return lax.all_to_all(x, axes, split_axis=0, concat_axis=0, tiled=True)


def on_device(
    hidden,
    norm_gain,
    query_weight,
    keyval_weight,
    output_weight,
    kv_cache,
    cache_lengths,
    next_source,
    block_ids,
):
    barrier = lax.optimization_barrier
    dp, tensor = lax.axis_size("dp"), lax.axis_size("tensor")
    rows, width = hidden.shape
    depth = width // dp
    group = block_ids.shape[0]
    mine = lax.axis_index("dp")

    arrived = exchange(prepare(block_ids, hidden, dp), "dp")

    block_rows = next_source.shape[1]
    piece_rows = block_rows // dp
    tile_cols = next_source.shape[2] // tensor
    slabs = next_source.reshape(dp, piece_rows, tensor, tile_cols).transpose(0, 2, 1, 3)
    slabs, arrived = barrier((slabs.reshape(dp * tensor, piece_rows, tile_cols), arrived))
    spread = exchange(slabs, ("dp", "tensor"))

    stream = hidden.astype(jnp.float32)
    meansq = jnp.mean(stream * stream, axis=-1, keepdims=True)
    row_scale = lax.rsqrt(meansq + 1e-05)
    gain = lax.dynamic_slice(norm_gain, (mine * depth,), (depth,))
    pieces = (
        arrived[:, :, :depth].reshape(dp * rows, depth).astype(jnp.float32)
        * gain.astype(jnp.float32)
    ).astype(jnp.bfloat16)
    flat_kv = keyval_weight.reshape(keyval_weight.shape[0], -1)
    partial = jnp.concatenate(
        [
            jnp.dot(pieces, query_weight, preferred_element_type=jnp.float32).astype(jnp.bfloat16),
            jnp.dot(pieces, flat_kv, preferred_element_type=jnp.float32).astype(jnp.bfloat16),
        ],
        axis=1,
    )
    cache = kv_cache.reshape(rows, kv_cache.shape[2], kv_cache.shape[3])
    ids = arrived[:, :, depth].reshape(dp * group).astype(jnp.int32)
    targets = jnp.stack([shifted(mine, step, 1) for step in STEPS])
    wanted = (targets[:, None] * group + jnp.arange(group, dtype=jnp.int32)[None, :]).reshape(-1)
    table = jnp.sum(
        jnp.where(
            ids[None, :] == wanted[:, None],
            jnp.arange(dp * group, dtype=jnp.int32)[None, :],
            0,
        ),
        axis=1,
    )
    owners = jnp.stack([shifted(mine, step, -1) for step in STEPS])
    partial, row_scale, table, owners, spread = barrier(
        (partial, row_scale, table, owners, spread)
    )

    terms = exchange(partial.reshape(dp, rows, -1), "dp")

    bounds = [0, 1 + len(ROUNDS[0])]
    for steps in ROUNDS[1:]:
        bounds.append(bounds[-1] + len(steps))
    tables = [table[group * i : group * j] for i, j in zip(bounds[:-1], bounds[1:])]
    kept, *ready = pick_slabs(tables[0], spread, bounds[1])
    landed = [kept] + [send(part, step) for part, step in zip(ready, ROUNDS[0])]

    def start_round(number, anchor):
        count = len(ROUNDS[number])
        anchor, *ready = barrier((anchor, *pick_slabs(tables[number], spread, count)))
        landed.extend(send(part, step) for part, step in zip(ready, ROUNDS[number]))
        return anchor

    def fence(name, anchor):
        count = FENCES.get(name, 0)
        anchor, *done = barrier((anchor, *landed[:count]))
        landed[:count] = done
        return anchor

    heads_out = attend(cache_lengths, terms, row_scale, cache)
    heads_out = fence("heads", heads_out)
    heads_out = start_round(1, heads_out)
    all_heads = exchange(heads_out, "dp")
    outbound = project_out(all_heads.reshape(dp * rows, -1), output_weight, dp, tensor)
    chunk = outbound.shape[3]
    outbound = outbound.reshape(dp * tensor, rows, chunk)
    outbound = fence("outbound", outbound)
    outbound = start_round(2, outbound)
    terms = exchange(outbound, ("dp", "tensor"))
    summed = sum_over_tensor(terms.reshape(dp, tensor, rows, chunk))
    summed = fence("summed", summed)
    placed = place_parts(owners[:EARLY], landed[:EARLY], dp)
    summed, placed = barrier((summed, placed))
    summed = start_round(3, summed)
    chunks = exchange(summed, "tensor")
    placed = place_parts(owners[EARLY:], landed[EARLY:], dp, placed)
    chunks, placed = barrier((chunks, placed))
    mixed = mix(hidden, chunks)

    next_weight = placed.reshape(group * block_rows, tile_cols)
    return (mixed, next_weight)


def solution(mesh):
    return jax.shard_map(
        on_device,
        mesh=mesh,
        in_specs=(
            P("dp", None),
            P(),
            P("dp", "tensor"),
            P("dp", "tensor", None),
            P("tensor", "dp"),
            P("dp", "tensor", None, None),
            P("dp"),
            P(("dp", "tensor"), None, None),
            P("dp"),
        ),
        out_specs=(P("dp", None), P("dp", "tensor")),
        check_vma=False,
    )
```

```python
import jax
import jax.numpy as jnp
from jax import lax
from jax.experimental import pallas as pl
from jax.experimental.pallas import tpu as pltpu
from jax.sharding import PartitionSpec as P

ANY = pl.BlockSpec(memory_space=pl.ANY)
HBM = pl.BlockSpec(memory_space=pltpu.HBM)
VMEM = pl.BlockSpec(memory_space=pltpu.VMEM)
SMEM = pl.BlockSpec(memory_space=pltpu.SMEM)
LANES = 128


def cost(flops, bytes_accessed):
    return pl.CostEstimate(flops=flops, bytes_accessed=bytes_accessed, transcendentals=0)


def prep_kernel(ids_ref, hidden_ref, out_ref):
    parts, rows, wide = out_ref.shape
    depth = wide - LANES
    row = lax.broadcasted_iota(jnp.int32, (rows, LANES), 0)
    numbers = jnp.zeros((rows, LANES), jnp.int32)
    for i in range(rows):
        numbers = jnp.where(row == i, ids_ref[i], numbers)
    numbers = numbers.astype(jnp.float32).astype(out_ref.dtype)
    for m in range(parts):
        out_ref[m, :, :depth] = hidden_ref[:, m * depth : (m + 1) * depth]
        out_ref[m, :, depth:] = numbers


def prepare(ids, hidden, parts):
    rows, width = hidden.shape
    return pl.pallas_call(
        prep_kernel,
        out_shape=jax.ShapeDtypeStruct((parts, rows, width // parts + LANES), hidden.dtype),
        in_specs=[SMEM, VMEM],
        out_specs=VMEM,
        cost_estimate=cost(0, 4 * hidden.size),
        name="prepare",
    )(ids, hidden)


def attend_kernel(
    lengths_ref, terms_ref, scale_ref, cache_ref, out_ref,
    query_ref, score_ref, weight_ref, sums_ref,
):
    copies, rows, query_cols = out_ref.shape
    length, head_dim = cache_ref.shape[1], cache_ref.shape[2] // 2
    heads = query_cols // head_dim
    total = terms_ref[0].astype(jnp.float32)
    for s in range(1, terms_ref.shape[0]):
        total = total + terms_ref[s].astype(jnp.float32)
    total = (total * scale_ref[...]).astype(jnp.bfloat16).astype(jnp.float32)
    for h in range(heads):
        query_ref[:, h, :] = total[:, h * head_dim : (h + 1) * head_dim]
    new_key = total[:, query_cols : query_cols + head_dim]
    new_value = total[:, query_cols + head_dim :]
    position = lax.broadcasted_iota(jnp.int32, (heads, length), 1)
    score_scale = head_dim ** (-0.5)
    for r in range(rows):
        scores = lax.dot_general(
            query_ref[r].astype(jnp.bfloat16),
            cache_ref[r, :, :head_dim],
            (((1,), (1,)), ((), ())),
            preferred_element_type=jnp.float32,
        )
        score_ref[r] = jnp.where(position < lengths_ref[r], scores * score_scale, -jnp.inf)
    self_score = jnp.sum(query_ref[...] * new_key[:, None, :], axis=2, keepdims=True) * score_scale
    scores = score_ref[...]
    highest = jnp.maximum(jnp.max(scores, axis=2, keepdims=True), self_score)
    expo = jnp.exp(scores - highest)
    self_expo = jnp.exp(self_score - highest)
    denominator = jnp.sum(expo, axis=2, keepdims=True) + self_expo
    weight_ref[...] = (expo / denominator).astype(jnp.bfloat16)
    self_weight = (self_expo / denominator).astype(jnp.bfloat16).astype(jnp.float32)
    sums_ref[...] = self_weight * new_value[:, None, :]
    for r in range(rows):
        sums_ref[r] += jnp.dot(
            weight_ref[r], cache_ref[r, :, head_dim:], preferred_element_type=jnp.float32
        )
    for h in range(heads):
        head = sums_ref[:, h, :].astype(out_ref.dtype)
        for copy in range(copies):
            out_ref[copy, :, h * head_dim : (h + 1) * head_dim] = head


def attend(lengths, terms, row_scale, cache):
    copies, rows, cols = terms.shape
    _, length, twice = cache.shape
    head_dim = twice // 2
    query_cols = cols - twice
    heads = query_cols // head_dim
    return pl.pallas_call(
        attend_kernel,
        out_shape=jax.ShapeDtypeStruct((copies, rows, query_cols), jnp.bfloat16),
        in_specs=[SMEM, VMEM, VMEM, VMEM],
        out_specs=VMEM,
        scratch_shapes=[
            pltpu.VMEM((rows, heads, head_dim), jnp.float32),
            pltpu.VMEM((rows, heads, length), jnp.float32),
            pltpu.VMEM((rows, heads, length), jnp.bfloat16),
            pltpu.VMEM((rows, heads, head_dim), jnp.float32),
        ],
        compiler_params=pltpu.CompilerParams(vmem_limit_bytes=16 << 20),
        cost_estimate=cost(4 * cache.size * heads, 2 * cache.size),
        name="attend",
    )(lengths, terms, row_scale, cache)


def output_kernel(heads_ref, weight_ref, out_ref):
    parts, chunks, rows, chunk = out_ref.shape
    step = 2 * chunk
    for j in range(chunks // 2):
        product = jnp.dot(
            heads_ref[...],
            weight_ref[:, j * step : (j + 1) * step],
            preferred_element_type=jnp.float32,
        )
        for k in range(2):
            tile = product[:, k * chunk : (k + 1) * chunk].reshape(parts, rows, chunk)
            out_ref[:, 2 * j + k] = tile.astype(out_ref.dtype)


def project_out(heads, weight, parts, chunks):
    rows, cols = heads.shape[0], weight.shape[1]
    return pl.pallas_call(
        output_kernel,
        out_shape=jax.ShapeDtypeStruct(
            (parts, chunks, rows // parts, cols // chunks), jnp.bfloat16
        ),
        in_specs=[VMEM, VMEM],
        out_specs=VMEM,
        compiler_params=pltpu.CompilerParams(vmem_limit_bytes=16 << 20),
        cost_estimate=cost(2 * rows * weight.size, 2 * weight.size),
        name="project_out",
    )(heads, weight)


def pick_kernel(table_ref, src_ref, *refs):
    *out_refs, sem = refs
    count, _, width = out_refs[0].shape
    for j, out_ref in enumerate(out_refs):
        for i in range(count):
            pltpu.make_async_copy(
                src_ref.at[table_ref[j * count + i], :, pl.ds(0, width)], out_ref.at[i], sem.at[j]
            ).start()
    for j, out_ref in enumerate(out_refs):
        pltpu.make_async_copy(out_ref, out_ref, sem.at[j]).wait()


def pick_slabs(table, slabs, parts):
    count = table.shape[0] // parts
    shape = (count, slabs.shape[1], slabs.shape[2])
    return pl.pallas_call(
        pick_kernel,
        out_shape=[jax.ShapeDtypeStruct(shape, slabs.dtype)] * parts,
        in_specs=[SMEM, HBM],
        out_specs=[VMEM] * parts,
        scratch_shapes=[pltpu.SemaphoreType.DMA((parts,))],
        compiler_params=pltpu.CompilerParams(vmem_limit_bytes=16 << 20),
        cost_estimate=cost(0, 4 * parts * count * slabs[0].size),
        name="pick_slabs",
    )(table, slabs)


def place_kernel(owner_ref, *refs):
    *refs, dst_ref, sem = refs
    part_refs = [ref for ref in refs if ref.shape != dst_ref.shape]
    copies = [
        pltpu.make_async_copy(part_ref, dst_ref.at[:, owner_ref[j]], sem.at[j])
        for j, part_ref in enumerate(part_refs)
    ]
    for copy in copies:
        copy.start()
    for copy in copies:
        copy.wait()


def place_parts(owners, parts, count, into=None):
    group, r, c = parts[0].shape
    held = [] if into is None else [into]
    return pl.pallas_call(
        place_kernel,
        out_shape=jax.ShapeDtypeStruct((group, count, r, c), parts[0].dtype),
        in_specs=[SMEM] + [VMEM] * len(parts) + [ANY] * len(held),
        out_specs=ANY,
        input_output_aliases={1 + len(parts): 0} if held else {},
        scratch_shapes=[pltpu.SemaphoreType.DMA((len(parts),))],
        compiler_params=pltpu.CompilerParams(vmem_limit_bytes=16 << 20),
        cost_estimate=pl.CostEstimate(
            flops=0, bytes_accessed=4 * len(parts) * parts[0].size, transcendentals=0
        ),
        name="place_parts",
    )(owners, *parts, *held)


ROUNDS = (
    ((0, 1, 0), (1, 3, 1)),
    ((0, 2, 0), (1, 0, 0), (0, 0, 1), (1, 1, 0), (0, 3, 0), (0, 2, 1)),
    ((1, 0, 1), (0, 1, 1), (1, 3, 0), (1, 1, 1)),
    ((0, 3, 1), (1, 2, 0), (1, 2, 1)),
)
STEPS = ((0, 0, 0),) + tuple(step for steps in ROUNDS for step in steps)
FENCES = {'heads': 3}
EARLY = 9


def shifted(index, step, sign):
    y_lo, x, core = index // 8, index // 2 % 4, index % 2
    return ((y_lo + step[0]) % 2 * 4 + (x + sign * step[1]) % 4) * 2 + (core + step[2]) % 2


def send(part, step):
    return lax.ppermute(part, "dp", [(s, shifted(s, step, 1)) for s in range(16)])


def sum_kernel(terms_ref, out_ref):
    for m in range(terms_ref.shape[0]):
        total = terms_ref[m, 0].astype(jnp.float32)
        for t in range(1, terms_ref.shape[1]):
            total = total + terms_ref[m, t].astype(jnp.float32)
        total = total.astype(out_ref.dtype)
        for copy in range(out_ref.shape[0]):
            out_ref[copy, m] = total


def sum_over_tensor(terms):
    dp, tensor, rows, chunk = terms.shape
    return pl.pallas_call(
        sum_kernel,
        out_shape=jax.ShapeDtypeStruct((tensor, dp, rows, chunk), terms.dtype),
        in_specs=[VMEM],
        out_specs=VMEM,
        cost_estimate=cost(terms.size, 4 * terms.size),
        name="sum_over_tensor",
    )(terms)


def mix_kernel(hidden_ref, chunks_ref, out_ref):
    tensor, dp, _, chunk = chunks_ref.shape
    for m in range(dp):
        for t in range(tensor):
            columns = slice((m * tensor + t) * chunk, (m * tensor + t + 1) * chunk)
            out_ref[:, columns] = (
                hidden_ref[:, columns].astype(jnp.float32)
                + chunks_ref[t, m].astype(jnp.float32)
            ).astype(out_ref.dtype)


def mix(hidden, chunks):
    return pl.pallas_call(
        mix_kernel,
        out_shape=jax.ShapeDtypeStruct(hidden.shape, hidden.dtype),
        in_specs=[VMEM, VMEM],
        out_specs=VMEM,
        cost_estimate=cost(hidden.size, 6 * hidden.size),
        name="mix",
    )(hidden, chunks)


def exchange(x, axes):
    return lax.all_to_all(x, axes, split_axis=0, concat_axis=0, tiled=True)


def on_device(
    hidden,
    norm_gain,
    query_weight,
    keyval_weight,
    output_weight,
    kv_cache,
    cache_lengths,
    next_source,
    block_ids,
):
    barrier = lax.optimization_barrier
    dp, tensor = lax.axis_size("dp"), lax.axis_size("tensor")
    rows, width = hidden.shape
    depth = width // dp
    group = block_ids.shape[0]
    mine = lax.axis_index("dp")

    arrived = exchange(prepare(block_ids, hidden, dp), "dp")

    block_rows = next_source.shape[1]
    piece_rows = block_rows // dp
    tile_cols = next_source.shape[2] // tensor
    slabs = next_source.reshape(dp, piece_rows, tensor, tile_cols).transpose(0, 2, 1, 3)
    slabs, arrived = barrier((slabs.reshape(dp * tensor, piece_rows, tile_cols), arrived))
    spread = exchange(slabs, ("dp", "tensor"))

    stream = hidden.astype(jnp.float32)
    meansq = jnp.mean(stream * stream, axis=-1, keepdims=True)
    row_scale = lax.rsqrt(meansq + 1e-05)
    gain = lax.dynamic_slice(norm_gain, (mine * depth,), (depth,))
    pieces = (
        arrived[:, :, :depth].reshape(dp * rows, depth).astype(jnp.float32)
        * gain.astype(jnp.float32)
    ).astype(jnp.bfloat16)
    flat_kv = keyval_weight.reshape(keyval_weight.shape[0], -1)
    partial = jnp.concatenate(
        [
            jnp.dot(pieces, query_weight, preferred_element_type=jnp.float32).astype(jnp.bfloat16),
            jnp.dot(pieces, flat_kv, preferred_element_type=jnp.float32).astype(jnp.bfloat16),
        ],
        axis=1,
    )
    cache = kv_cache.reshape(rows, kv_cache.shape[2], kv_cache.shape[3])
    ids = arrived[:, :, depth].reshape(dp * group).astype(jnp.int32)
    targets = jnp.stack([shifted(mine, step, 1) for step in STEPS])
    wanted = (targets[:, None] * group + jnp.arange(group, dtype=jnp.int32)[None, :]).reshape(-1)
    table = jnp.sum(
        jnp.where(
            ids[None, :] == wanted[:, None],
            jnp.arange(dp * group, dtype=jnp.int32)[None, :],
            0,
        ),
        axis=1,
    )
    owners = jnp.stack([shifted(mine, step, -1) for step in STEPS])
    partial, row_scale, table, owners, spread = barrier(
        (partial, row_scale, table, owners, spread)
    )

    terms = exchange(partial.reshape(dp, rows, -1), "dp")

    bounds = [0, 1 + len(ROUNDS[0])]
    for steps in ROUNDS[1:]:
        bounds.append(bounds[-1] + len(steps))
    tables = [table[group * i : group * j] for i, j in zip(bounds[:-1], bounds[1:])]
    kept, *ready = pick_slabs(tables[0], spread, bounds[1])
    landed = [kept] + [send(part, step) for part, step in zip(ready, ROUNDS[0])]

    def start_round(number, anchor):
        count = len(ROUNDS[number])
        anchor, *ready = barrier((anchor, *pick_slabs(tables[number], spread, count)))
        landed.extend(send(part, step) for part, step in zip(ready, ROUNDS[number]))
        return anchor

    def fence(name, anchor):
        count = FENCES.get(name, 0)
        anchor, *done = barrier((anchor, *landed[:count]))
        landed[:count] = done
        return anchor

    heads_out = attend(cache_lengths, terms, row_scale, cache)
    heads_out = fence("heads", heads_out)
    heads_out = start_round(1, heads_out)
    all_heads = exchange(heads_out, "dp")
    outbound = project_out(all_heads.reshape(dp * rows, -1), output_weight, dp, tensor)
    chunk = outbound.shape[3]
    outbound = outbound.reshape(dp * tensor, rows, chunk)
    outbound = fence("outbound", outbound)
    outbound = start_round(2, outbound)
    terms = exchange(outbound, ("dp", "tensor"))
    summed = sum_over_tensor(terms.reshape(dp, tensor, rows, chunk))
    summed = fence("summed", summed)
    placed = place_parts(owners[:EARLY], landed[:EARLY], dp)
    summed, placed = barrier((summed, placed))
    summed = start_round(3, summed)
    chunks = exchange(summed, "tensor")
    placed = place_parts(owners[EARLY:], landed[EARLY:], dp, placed)
    chunks, placed = barrier((chunks, placed))
    mixed = mix(hidden, chunks)

    next_weight = placed.reshape(group * block_rows, tile_cols)
    return (mixed, next_weight)


def solution(mesh):
    return jax.shard_map(
        on_device,
        mesh=mesh,
        in_specs=(
            P("dp", None),
            P(),
            P("dp", "tensor"),
            P("dp", "tensor", None),
            P("tensor", "dp"),
            P("dp", "tensor", None, None),
            P("dp"),
            P(("dp", "tensor"), None, None),
            P("dp"),
        ),
        out_specs=(P("dp", None), P("dp", "tensor")),
        check_vma=False,
    )
```
